256 devices in a mesh: dp: 32 (over y, z), tensor: 8 (over x, core).
Axes of the slice: x: 4, y: 4, z: 8, core: 2. Of those that a mesh axis runs over, the one named last changes fastest.
Arguments:
- activations: bfloat16 [24576, 5120], P('dp'), may hold values from -6 to 6
- cotangent: bfloat16 [3, 24576, 5120], P(None, 'dp', 'tensor'), may hold values from -0.09375 to 0.09375
- projector: bfloat16 [3, 5120, 512], P(None, 'dp'), may hold values from -0.078125 to 0.078125
- first_moment: float32 [3, 512, 5120], P(None, 'dp', 'tensor'), may hold values from -6 to 6
- second_moment: float32 [3, 512, 5120], P(None, 'dp', 'tensor'), may hold values from 0.3 to 3
Outputs:
- new_first: float32 [3, 512, 5120], P(None, 'dp', 'tensor')
- new_second: float32 [3, 512, 5120], P(None, 'dp', 'tensor')
- update: bfloat16 [3, 5120, 5120], P(None, 'dp', 'tensor')
The draws below stay inside these ranges and needn't reach their ends.
All inputs are finite; a program needn't handle non-finite values.
Results may differ from the reference program's by a relative error of at most 0.005.
Values may be sent and summed in bfloat16 or wider, within the bound.
A program may use at most 128 MiB of HBM per device.

```python
import math
import jax
import jax.numpy as jnp
from jax import lax

D = 5120
RANK = 512
TOK_DEV = 768
TOKENS = 24576
N_DP = 32


def steps_of(own_key, shape, pieces, least, top_value):
    gain, own = 1.0, jax.random.fold_in(own_key, 6)
    for axis_at, blocks in pieces:
        heights = jnp.exp(jax.random.uniform(jax.random.fold_in(own, axis_at), (blocks,), jnp.float32, least / len(pieces), top_value / len(pieces)))
        gain = gain * jnp.repeat(heights, shape[axis_at] // blocks).reshape([-1 if axis == axis_at else 1 for axis in range(len(shape))])
    return gain


def scatter_about(own_key, dims, spread, most, split=(), dtype=jnp.bfloat16):
    values = jax.random.normal(own_key, dims, jnp.float32) * spread
    if len(split) > 0:
        values = steps_of(own_key, dims, split, -0.22, 0.18) * values
    return jnp.clip(values, min=-most, max=most).astype(dtype)


def setup_inputs(seed: int = 0) -> dict:
    key_list = jax.random.split(jax.random.key(seed), 6)
    return {
        "activations": scatter_about(key_list[0], (TOKENS, D), 1.0, 6.0, ((0, 32),)),
        "cotangent": scatter_about(key_list[1], (3, TOKENS, D), (1.0 / (TOK_DEV * N_DP) ** 0.5), 0.09375, ((1, 32), (2, 8))),
        "projector": scatter_about(key_list[2], (3, D, RANK), D ** -0.5, 0.078125, ((1, 32),)),
        "first_moment": scatter_about(key_list[3], (3, RANK, D), 1.0, 6.0, ((1, 32), (2, 8)), jnp.float32),
        "second_moment": jnp.clip(jnp.exp(math.log(3.0) - 2.3025851 * jax.random.uniform(key_list[4], (3, RANK, D), jnp.float32) ** steps_of(key_list[4], (3, RANK, D), ((1, 32), (2, 8)), -0.2, 0.2)), 0.3, 3.0),
    }


beta_one = 0.9
beta_two = 0.95
adam_eps = 1e-08
bias_one = 1.0 - 0.9 ** 10
bias_two = 1.0 - 0.95 ** 10

def reference(activations, cotangent, projector, first_moment, second_moment):
    firsts = []
    seconds = []
    updates = []
    for matrix in range(3):
        lowered = jnp.dot(activations, projector[matrix], preferred_element_type=jnp.float32)
        grad_low = jnp.einsum('ts,tc->sc', lowered, cotangent[matrix].astype(jnp.float32), precision=lax.Precision.HIGHEST)
        fresh_first = beta_one * first_moment[matrix] + (1.0 - beta_one) * grad_low
        fresh_second = beta_two * second_moment[matrix] + (1.0 - beta_two) * grad_low * grad_low
        low_step = (fresh_first / bias_one / (jnp.sqrt(fresh_second / bias_two) + adam_eps)).astype(jnp.bfloat16)
        updates.append(jnp.dot(projector[matrix], low_step, preferred_element_type=jnp.float32).astype(jnp.bfloat16))
        firsts.append(fresh_first)
        seconds.append(fresh_second)
    return (jnp.stack(firsts), jnp.stack(seconds), jnp.stack(updates))
```

```python
import jax
import jax.numpy as jnp
from jax import lax
from jax.sharding import PartitionSpec as P

beta_one = 0.9
beta_two = 0.95
adam_eps = 1e-08
bias_one = 1.0 - 0.9**10
bias_two = 1.0 - 0.95**10


def on_device(activations, cotangent, projector, first_moment, second_moment):
    parts = lax.axis_size("tensor")
    width = projector.shape[2] // parts
    mine = lax.dynamic_slice_in_dim(projector, lax.axis_index("tensor") * width, width, axis=2)
    gathered = lax.all_gather(mine, "dp", axis=1, tiled=True)
    lowered = jnp.einsum(
        "tr,krs->kts", activations, gathered, preferred_element_type=jnp.float32
    ).astype(jnp.bfloat16)
    lowered = lax.all_gather(lowered, "tensor", axis=2, tiled=True)
    grad_local = jnp.einsum("kts,ktc->ksc", lowered, cotangent, preferred_element_type=jnp.float32)
    grad_owned = lax.psum_scatter(grad_local, "dp", scatter_dimension=1, tiled=True)
    fresh_first = beta_one * first_moment + (1.0 - beta_one) * grad_owned
    fresh_second = beta_two * second_moment + (1.0 - beta_two) * grad_owned * grad_owned
    low_step = (fresh_first / bias_one / (jnp.sqrt(fresh_second / bias_two) + adam_eps)).astype(
        jnp.bfloat16
    )
    expanded = jnp.einsum(
        "krs,ksc->krc",
        projector,
        lax.all_gather(low_step, "dp", axis=1, tiled=True),
        preferred_element_type=jnp.float32,
    )
    return (fresh_first, fresh_second, expanded.astype(jnp.bfloat16))


def solution(mesh):
    placed = (
        P("dp", None),
        P(None, "dp", "tensor"),
        P(None, "dp", None),
        P(None, "dp", "tensor"),
        P(None, "dp", "tensor"),
    )
    return jax.shard_map(
        on_device,
        mesh=mesh,
        in_specs=placed,
        out_specs=(P(None, "dp", "tensor"), P(None, "dp", "tensor"), P(None, "dp", "tensor")),
        check_vma=False,
    )
```

```python
import jax
import jax.numpy as jnp
from jax import lax
from jax.experimental import pallas as pl
from jax.experimental.pallas import tpu as pltpu
from jax.sharding import PartitionSpec as P

beta_one = 0.9
beta_two = 0.95
adam_eps = 1e-08
bias_one = 1.0 - 0.9**10
bias_two = 1.0 - 0.95**10

MESH = pl.DeviceIdType.MESH
f32, bf16 = jnp.float32, jnp.bfloat16
NK, NY, NZ, NX = 3, 4, 8, 4
TOK, HALF = 768, 384
ROWS, SHARE = 160, 80
BIG, SMALL = 64, 16
SLAB = NZ * ROWS
LANES = 128
COLS, WIDE = 640, 512
OWN = 16

Z_P0, Z_P1, Z_R0, Z_R1, Z_L0, Z_L1 = range(6)
Y_P0, Y_P1, Y_R0, Y_R1, Y_L0, Y_L1 = range(6)


def kernel(
    p_ref, m1_ref, m2_ref, a_hbm, g_hbm,
    nf_ref, ns_ref, u_ref,
    pg, av, gv, acc, lt, gr, rb0, rb1, s0, s1, q0, q1, lg,
    zs, zr, ys, yr, cs, cr, xs, xr, ds, dr, lsem,
):
    dp, tensor = lax.axis_index("dp"), lax.axis_index("tensor")
    y, z, x, c = dp // NZ, dp % NZ, tensor // 2, tensor % 2

    load_a = pltpu.make_async_copy(
        a_hbm.at[pl.ds(pl.multiple_of(c * HALF, HALF), HALF)], av, lsem.at[0]
    )
    load_g = pltpu.make_async_copy(g_hbm, gv, lsem.at[1])

    def at_z(d):
        return (y * NZ + (z + d) % NZ, tensor)

    def at_y(d):
        return (((y + d) % NY) * NZ + z, tensor)

    def at_x(d):
        return (dp, ((x + d) % NX) * 2 + c)

    partner = (dp, x * 2 + (1 - c))

    barrier = pltpu.get_barrier_semaphore()

    def greet(who):
        pl.semaphore_signal(barrier, inc=1, device_id=who, device_id_type=MESH)

    for d in range(1, NZ):
        greet(at_z(d))
    for d in range(1, NY):
        greet(at_y(d))
    for d in range(1, NX):
        greet(at_x(d))
    greet(partner)
    load_a.start()
    load_g.start()

    rows0 = pl.ds(pl.multiple_of(c * SHARE, 16), BIG)
    rows1 = pl.ds(pl.multiple_of(c * SHARE + BIG, 16), SMALL)
    share = pl.ds(pl.multiple_of(c * SHARE, 16), SHARE)
    mine = pl.ds(pl.multiple_of(x * LANES, LANES), LANES)
    toks = pl.ds(pl.multiple_of(c * HALF, HALF), HALF)
    low, high = pl.ds(0, WIDE), pl.ds(WIDE, COLS - WIDE)

    def copy(src, dst, send, recv, who):
        return pltpu.make_async_remote_copy(
            src_ref=src, dst_ref=dst, send_sem=send, recv_sem=recv,
            device_id=who, device_id_type=MESH,
        )

    def z_refs(kind, k, d):
        to = (z + d) % NZ
        if kind == Z_P0:
            return p_ref.at[k, rows0, mine], pg.at[k, y, z, rows0]
        if kind == Z_P1:
            here = pg.at[k, :, z, rows1]
            return here, here
        if kind == Z_R0:
            return s0.at[k, to], q0.at[k, d]
        if kind == Z_R1:
            return gr.at[k, :, to, :, high], rb1.at[k, d]
        if kind == Z_L0:
            here = lg.at[k, y, z, :, low]
            return here, here
        here = lg.at[k, :, z, :, high]
        return here, here

    def y_refs(kind, k, d):
        to = (y + d) % NY
        if kind == Y_P0:
            here = pg.at[k, y, :, rows0]
            return here, here
        if kind == Y_P1:
            return p_ref.at[k, rows1, mine], pg.at[k, y, z, rows1]
        if kind == Y_R0:
            return gr.at[k, to, :, :, low], rb0.at[k, d]
        if kind == Y_R1:
            return s1.at[k, to], q1.at[k, d]
        if kind == Y_L0:
            here = lg.at[k, y, :, :, low]
            return here, here
        here = lg.at[k, y, z, :, high]
        return here, here

    def z_copy(kind, k, d):
        src, dst = z_refs(kind, k, d)
        return copy(src, dst, zs.at[kind, k, d], zr.at[kind, k, d], at_z(d))

    def y_copy(kind, k, d):
        src, dst = y_refs(kind, k, d)
        return copy(src, dst, ys.at[kind, k, d], yr.at[kind, k, d], at_y(d))

    def c_copy(k, i):
        if isinstance(i, int) and i == NY:
            here = pg.at[k, :, :, rows1]
        else:
            here = pg.at[k, (y + NY - i) % NY, :, rows0]
        return copy(here, here, cs.at[k, i], cr.at[k, i], partner)

    def x_copy(k, d):
        here = lt.at[k, x, :, toks]
        return copy(here, here, xs.at[k, d], xr.at[k, d], at_x(d))

    def d_copy(k, d):
        here = lt.at[k, (x + NX - d) % NX, :, toks]
        return copy(here, here, ds.at[k, d], dr.at[k, d], partner)

    def each(n, act):
        def body(d, carry):
            act(d)
            return carry

        lax.fori_loop(1, n, body, 0)

    def z_start(kind, k):
        each(NZ, lambda d: z_copy(kind, k, d).start())

    def z_arrive(kind, k):
        each(NZ, lambda d: z_copy(kind, k, d).wait_recv())

    def y_start(kind, k):
        each(NY, lambda d: y_copy(kind, k, d).start())

    def y_arrive(kind, k):
        each(NY, lambda d: y_copy(kind, k, d).wait_recv())

    def gather_first(k):
        z_start(Z_P0, k)
        y_start(Y_P1, k)
        pg[k, y, z, share] = p_ref[k, share, mine]

    def gather_second(k):
        y_arrive(Y_P1, k)
        z_start(Z_P1, k)
        z_arrive(Z_P0, k)
        y_start(Y_P0, k)
        c_copy(k, 0).start()

    def add_slab(k, d, first=False):
        at = (y + NY - d) % NY
        part = jnp.dot(
            av[:, pl.ds(pl.multiple_of(at * SLAB, LANES), SLAB)],
            pg[k, at].reshape(SLAB, LANES),
            preferred_element_type=f32,
        )
        acc[...] = part if first else acc[...] + part

    def lower(k):
        z_arrive(Z_P1, k)
        c_copy(k, NY).start()
        if k == 0:
            load_a.wait()
        c_copy(k, NY).wait_recv()
        c_copy(k, 0).wait_recv()
        add_slab(k, 0, True)
        y_copy(Y_P0, k, 1).wait_recv()
        c_copy(k, 1).start()
        y_copy(Y_P0, k, 3).wait_recv()
        c_copy(k, 3).start()
        c_copy(k, 1).wait_recv()
        add_slab(k, 1)
        y_copy(Y_P0, k, 2).wait_recv()
        c_copy(k, 2).start()
        c_copy(k, 3).wait_recv()
        add_slab(k, 3)
        c_copy(k, 2).wait_recv()
        add_slab(k, 2)
        lt[k, x, :, toks] = acc[...].T.astype(bf16)
        each(NX, lambda d: x_copy(k, d).start())
        d_copy(k, 0).start()

    def grad_slab(k, d):
        at = (x + NX - d) % NX
        part = jnp.dot(lt[k, at], gv[k], preferred_element_type=f32)
        gr[k, at] = part.astype(bf16).reshape(NZ, OWN, COLS)

        @pl.when(at != y)
        def _():
            y_copy(Y_R0, k, (at + NY - y) % NY).start()

    def grad(k):
        if k == 0:
            load_g.wait()
        d_copy(k, 0).wait_recv()
        grad_slab(k, 0)
        x_copy(k, 1).wait_recv()
        d_copy(k, 1).start()
        x_copy(k, 3).wait_recv()
        d_copy(k, 3).start()
        d_copy(k, 1).wait_recv()
        grad_slab(k, 1)
        x_copy(k, 2).wait_recv()
        d_copy(k, 2).start()
        d_copy(k, 3).wait_recv()
        grad_slab(k, 3)
        d_copy(k, 2).wait_recv()
        grad_slab(k, 2)
        z_start(Z_R1, k)

    def reduce_second(k):
        z_arrive(Z_R1, k)
        total = gr[k, :, z, :, high].astype(f32)
        for d in range(1, NZ):
            total += rb1[k, d].astype(f32)
        s1[k] = total.astype(bf16)
        y_start(Y_R1, k)
        y_arrive(Y_R0, k)
        total = gr[k, y, :, :, low].astype(f32)
        for d in range(1, NY):
            total += rb0[k, d].astype(f32)
        s0[k] = total.astype(bf16)
        z_start(Z_R0, k)

    def step(k, cols, grad_owned):
        first = beta_one * m1_ref[k, :, cols] + (1.0 - beta_one) * grad_owned
        second = beta_two * m2_ref[k, :, cols] + (1.0 - beta_two) * grad_owned * grad_owned
        nf_ref[k, :, cols] = first
        ns_ref[k, :, cols] = second
        low_step = first / bias_one / (jnp.sqrt(second / bias_two) + adam_eps)
        lg[k, y, z, :, cols] = low_step.astype(bf16)

    def moments(k):
        y_arrive(Y_R1, k)
        total = s1[k, y].astype(f32)
        for d in range(1, NY):
            total += q1[k, d].astype(f32)
        step(k, high, total)
        y_start(Y_L1, k)
        z_arrive(Z_R0, k)
        total = s0[k, z].astype(f32)
        for d in range(1, NZ):
            total += q0[k, d].astype(f32)
        step(k, low, total)
        z_start(Z_L0, k)

    def spread_second(k):
        y_arrive(Y_L1, k)
        z_start(Z_L1, k)
        z_arrive(Z_L0, k)
        y_start(Y_L0, k)

    def update(k):
        z_arrive(Z_L1, k)
        y_arrive(Y_L0, k)
        whole = lg[k].reshape(NY * NZ * OWN, COLS)
        u_ref[k] = jnp.dot(p_ref[k], whole, preferred_element_type=f32).astype(bf16)

    pl.semaphore_wait(barrier, NZ - 1 + NY - 1 + NX - 1 + 1)

    for what, k in (
        (gather_first, 0), (gather_first, 1), (gather_first, 2),
        (gather_second, 0), (gather_second, 1), (gather_second, 2),
        (lower, 0), (lower, 1), (grad, 0), (lower, 2), (grad, 1), (reduce_second, 0),
        (grad, 2), (moments, 0), (reduce_second, 1), (spread_second, 0),
        (moments, 1), (reduce_second, 2), (update, 0), (spread_second, 1),
        (moments, 2), (update, 1), (spread_second, 2), (update, 2),
    ):
        what(k)

    for k in range(NK):
        for kind in range(6):
            each(NZ, lambda d: z_copy(kind, k, d).wait_send())
            each(NY, lambda d: y_copy(kind, k, d).wait_send())
        for i in range(NY + 1):
            c_copy(k, i).wait_send()
        for d in range(NX):
            d_copy(k, d).wait_send()
        each(NX, lambda d: x_copy(k, d).wait_send())


def on_device(activations, cotangent, projector, first_moment, second_moment):
    vmem = pl.BlockSpec(memory_space=pltpu.VMEM)
    hbm = pl.BlockSpec(memory_space=pl.ANY)
    dma = pltpu.SemaphoreType.DMA
    return pl.pallas_call(
        kernel,
        out_shape=(
            jax.ShapeDtypeStruct((NK, OWN, COLS), f32),
            jax.ShapeDtypeStruct((NK, OWN, COLS), f32),
            jax.ShapeDtypeStruct((NK, ROWS, COLS), bf16),
        ),
        in_specs=[vmem, vmem, vmem, hbm, hbm],
        out_specs=(vmem, vmem, vmem),
        scratch_shapes=[
            pltpu.VMEM((NK, NY, NZ, ROWS, LANES), bf16),
            pltpu.VMEM((HALF, NY * SLAB), bf16),
            pltpu.VMEM((NK, TOK, COLS), bf16),
            pltpu.VMEM((HALF, LANES), f32),
            pltpu.VMEM((NK, NX, LANES, TOK), bf16),
            pltpu.VMEM((NK, NY, NZ, OWN, COLS), bf16),
            pltpu.VMEM((NK, NY, NZ, OWN, WIDE), bf16),
            pltpu.VMEM((NK, NZ, NY, OWN, COLS - WIDE), bf16),
            pltpu.VMEM((NK, NZ, OWN, WIDE), bf16),
            pltpu.VMEM((NK, NY, OWN, COLS - WIDE), bf16),
            pltpu.VMEM((NK, NZ, OWN, WIDE), bf16),
            pltpu.VMEM((NK, NY, OWN, COLS - WIDE), bf16),
            pltpu.VMEM((NK, NY, NZ, OWN, COLS), bf16),
            dma((6, NK, NZ)), dma((6, NK, NZ)),
            dma((6, NK, NY)), dma((6, NK, NY)),
            dma((NK, NY + 1)), dma((NK, NY + 1)),
            dma((NK, NX)), dma((NK, NX)),
            dma((NK, NX)), dma((NK, NX)),
            dma((2,)),
        ],
        compiler_params=pltpu.CompilerParams(
            collective_id=0, has_side_effects=True, vmem_limit_bytes=44 * 2**20
        ),
        name="galore_step",
    )(projector, first_moment, second_moment, activations, cotangent)


def solution(mesh):
    placed = (
        P("dp", None),
        P(None, "dp", "tensor"),
        P(None, "dp", None),
        P(None, "dp", "tensor"),
        P(None, "dp", "tensor"),
    )
    return jax.shard_map(
        on_device,
        mesh=mesh,
        in_specs=placed,
        out_specs=(P(None, "dp", "tensor"), P(None, "dp", "tensor"), P(None, "dp", "tensor")),
        check_vma=False,
    )
```

```python
import jax
import jax.numpy as jnp
from jax import lax
from jax.experimental import pallas as pl
from jax.experimental.pallas import tpu as pltpu
from jax.sharding import PartitionSpec as P

beta_one = 0.9
beta_two = 0.95
adam_eps = 1e-08
bias_one = 1.0 - 0.9**10
bias_two = 1.0 - 0.95**10

MESH = pl.DeviceIdType.MESH
f32, bf16 = jnp.float32, jnp.bfloat16
NK, NY, NZ, NX = 3, 4, 8, 4
TOK, HALF = 768, 384
ROWS, SHARE = 160, 80
BIG, SMALL = 64, 16
SLAB = NZ * ROWS
LANES = 128
COLS, WIDE = 640, 512
OWN = 16

Z_ORDER = (1, 7, 2, 6, 3, 5, 4)
Z_COME = (1, 7, 2, 6, 3, 5, 4)
Z_P0, Z_P1, Z_R0, Z_R1, Z_L0, Z_L1 = range(6)
Y_P0, Y_P1, Y_R0, Y_R1, Y_L0, Y_L1, Y_R2, Y_U = range(8)


def kernel(
    p_hbm, m1_hbm, m2_hbm, a_hbm, g_hbm,
    nf_ref, ns_ref, u_ref,
    p_ref, m1_ref, m2_ref, pg, av, gv, acc, lt, gr, rb0, rb1, s0, s1, q0, q1, lown, la, lb, p4, uq,
    zs, zr, zpr, ys, yr, ypr, cs, cr, xs, xr, ds, dr, ps, pr, es, er, lsem,
):
    dp, tensor = lax.axis_index("dp"), lax.axis_index("tensor")
    y, z, x, c = dp // NZ, dp % NZ, tensor // 2, tensor % 2

    load_a = pltpu.make_async_copy(
        a_hbm.at[pl.ds(pl.multiple_of(c * HALF, HALF), HALF)], av, lsem.at[0]
    )
    load_g = pltpu.make_async_copy(g_hbm, gv, lsem.at[1])
    load_p = pltpu.make_async_copy(p_hbm, p_ref, lsem.at[2])
    load_m1 = pltpu.make_async_copy(m1_hbm, m1_ref, lsem.at[3])
    load_m2 = pltpu.make_async_copy(m2_hbm, m2_ref, lsem.at[4])
    load_p.start()

    zt = [lax.rem(z + d, NZ) for d in range(NZ)]
    yt = [lax.rem(y + d, NY) for d in range(NY)]
    xt = [lax.rem(x + d, NX) for d in range(NX)]
    at_z = [(y * NZ + zt[d], tensor) for d in range(NZ)]
    at_y = [(yt[d] * NZ + z, tensor) for d in range(NY)]
    at_x = [(dp, xt[d] * 2 + c) for d in range(NX)]
    partner = (dp, x * 2 + (1 - c))

    barrier = pltpu.get_barrier_semaphore()

    def greet(who):
        pl.semaphore_signal(barrier, inc=1, device_id=who, device_id_type=MESH)

    for d in range(1, NZ):
        greet(at_z[d])
    for d in range(1, NY):
        greet(at_y[d])
    for d in range(1, NX):
        greet(at_x[d])
    greet(partner)
    load_a.start()
    load_g.start()
    load_m1.start()
    load_m2.start()

    rows0 = pl.ds(pl.multiple_of(c * SHARE, 16), BIG)
    rows1 = pl.ds(pl.multiple_of(c * SHARE + BIG, 16), SMALL)
    share = pl.ds(pl.multiple_of(c * SHARE, 16), SHARE)
    mine = pl.ds(pl.multiple_of(x * LANES, LANES), LANES)
    toks = pl.ds(pl.multiple_of(c * HALF, HALF), HALF)
    low, high = pl.ds(0, WIDE), pl.ds(WIDE, COLS - WIDE)

    def copy(src, dst, send, recv, who):
        return pltpu.make_async_remote_copy(
            src_ref=src, dst_ref=dst, send_sem=send, recv_sem=recv,
            device_id=who, device_id_type=MESH,
        )

    def z_copy(kind, k, d):
        to = zt[d]
        if kind == Z_P0:
            src, dst = p_ref.at[k, rows0, mine], pg.at[k, y, z, rows0]
        elif kind == Z_P1:
            src = dst = pg.at[k, :, z, rows1]
        elif kind == Z_R1:
            src, dst = gr.at[k, :, to, :, high], rb1.at[k, d]
        elif kind == Z_L0:
            src = dst = la.at[k, :, z]
        else:
            src = dst = lb.at[k, y, z]
        recv = zpr.at[k, d] if kind == Z_P0 else zr.at[kind, k]
        return copy(src, dst, zs.at[kind, k], recv, at_z[d])

    def y_copy(kind, k, d):
        to = yt[d]
        if kind == Y_P1:
            src, dst = p_ref.at[k, rows1, mine], pg.at[k, y, z, rows1]
        elif kind == Y_R1:
            src, dst = s1.at[k, to], q1.at[k, d]
        elif kind == Y_L0:
            src, dst = lown.at[k, to], la.at[k, y, z]
        elif kind == Y_L1:
            src = dst = lb.at[k, y]
        else:
            quarter = pl.ds(pl.multiple_of(y * LANES, LANES), LANES)
            src, dst = uq.at[k, to], u_ref.at[k, :, quarter]
        return copy(src, dst, ys.at[kind, k], yr.at[kind, k], at_y[d])

    def y_block(k, at):
        here = pg.at[k, y, at, rows0]
        for d in (2, 1, 3):
            copy(here, here, ys.at[Y_P0, k], ypr.at[k, d], at_y[d]).start()

    def y_slab(k, d):
        here = pg.at[k, yt[(NY - d) % NY], :, rows0]
        return copy(here, here, ys.at[Y_P0, k], ypr.at[k, d], partner)

    def c_copy(k, i):
        here = pg.at[k, :, :, rows1] if i == NY else pg.at[k, yt[(NY - i) % NY], :, rows0]
        return copy(here, here, cs.at[k], cr.at[k, i], partner)

    def x_copy(k, d):
        here = lt.at[k, x, :, toks]
        return copy(here, here, xs.at[k], xr.at[k, d], at_x[d])

    def d_copy(k, d):
        here = lt.at[k, xt[(NX - d) % NX], :, toks]
        return copy(here, here, ds.at[k], dr.at[k, d], partner)

    def p_copy(k, d):
        return copy(pg.at[k, :, z, share], p4.at[k, :, share, mine], ps.at[k], pr.at[k], at_x[d])

    def e_copy(k):
        here = p4.at[k, :, share]
        return copy(here, here, es.at[k], er.at[k], partner)

    def z_all(kind, k):
        some = pl.ds(1, NZ - 1)
        whole = {
            Z_P0: pg.at[k, 0, some, pl.ds(0, BIG)],
            Z_P1: pg.at[k, :, some, rows1],
            Z_R0: q0.at[k, some],
            Z_R1: rb1.at[k, some],
            Z_L0: la.at[k, :, some],
            Z_L1: lb.at[k, y, some],
        }[kind]
        return copy(whole, whole, zs.at[kind, k], zr.at[kind, k], partner)

    def y_all(kind, k):
        some = pl.ds(1, NY - 1)
        whole = {
            Y_P0: pg.at[k, some, :, pl.ds(0, BIG)],
            Y_P1: pg.at[k, some, z, rows1],
            Y_R0: rb0.at[k, some, pl.ds(0, NZ // 2)],
            Y_R2: rb0.at[k, some, pl.ds(NZ // 2, NZ // 2)],
            Y_R1: q1.at[k, some],
            Y_L0: la.at[k, some, z],
            Y_L1: lb.at[k, some],
            Y_U: uq.at[k, some],
        }[kind]
        return copy(whole, whole, ys.at[kind, k], yr.at[kind, k], partner)

    def x_all(k):
        whole = lt.at[k, pl.ds(1, NX - 1), :, pl.ds(0, HALF)]
        return copy(whole, whole, xs.at[k], xr.at[k, 0], partner)

    def p_all(k):
        whole = pg.at[k, :, pl.ds(1, NX - 1), pl.ds(0, SHARE)]
        return copy(whole, whole, ps.at[k], pr.at[k], partner)

    def c_all(k):
        whole = pg.at[k, :, :, pl.ds(0, SHARE)]
        return copy(whole, whole, cs.at[k], cr.at[k, 0], partner)

    def d_all(k):
        whole = lt.at[k, :, :, pl.ds(0, HALF)]
        return copy(whole, whole, ds.at[k], dr.at[k, 0], partner)

    def z_start(kind, k):
        for d in Z_ORDER:
            z_copy(kind, k, d).start()

    def z_arrive(kind, k):
        z_all(kind, k).wait_recv()

    def y_start(kind, k):
        for d in (2, 1, 3):
            y_copy(kind, k, d).start()

    def y_arrive(kind, k):
        y_all(kind, k).wait_recv()

    def gather_first(k):
        if k:
            z_all(Z_P0, k - 1).wait_send()
        z_start(Z_P0, k)
        y_start(Y_P1, k)
        pg[k, y, z, share] = p_ref[k, share, mine]
        y_block(k, z)

    def gather_second(k):
        y_arrive(Y_P1, k)
        z_start(Z_P1, k)
        for d in Z_COME:
            z_copy(Z_P0, k, d).wait_recv()
            y_block(k, zt[NZ - d])
        c_copy(k, 0).start()

    def add_slab(k, d, first=False):
        at = yt[(NY - d) % NY]
        part = jnp.dot(
            av[:, pl.ds(pl.multiple_of(at * SLAB, LANES), SLAB)],
            pg[k, at].reshape(SLAB, LANES),
            preferred_element_type=f32,
        )
        acc[...] = part if first else acc[...] + part

    def lower(k):
        z_arrive(Z_P1, k)
        c_copy(k, NY).start()
        if k == 0:
            load_a.wait()
        c_copy(k, NY).wait_recv()
        c_copy(k, 0).wait_recv()
        add_slab(k, 0, True)
        y_slab(k, 1).wait_recv()
        c_copy(k, 1).start()
        y_slab(k, 3).wait_recv()
        c_copy(k, 3).start()
        c_copy(k, 1).wait_recv()
        add_slab(k, 1)
        y_slab(k, 2).wait_recv()
        c_copy(k, 2).start()
        c_copy(k, 3).wait_recv()
        add_slab(k, 3)
        c_copy(k, 2).wait_recv()
        add_slab(k, 2)
        lt[k, x, :, toks] = acc[...].T.astype(bf16)
        for d in (2, 1, 3):
            x_copy(k, d).start()
        d_copy(k, 0).start()

    def grad_slab(k, d):
        at = xt[(NX - d) % NX]
        part = jnp.dot(lt[k, at], gv[k], preferred_element_type=f32)
        gr[k, at] = part.astype(bf16).reshape(NZ, OWN, COLS)

        @pl.when(at != y)
        def _():
            d = lax.rem(at + NY - y, NY)
            for kind, some in ((Y_R0, pl.ds(0, NZ // 2)), (Y_R2, pl.ds(NZ // 2, NZ // 2))):
                src, dst = gr.at[k, at, some, :, low], rb0.at[k, d, some]
                copy(src, dst, ys.at[kind, k], yr.at[kind, k], (at * NZ + z, tensor)).start()

    def grad(k):
        if k == 0:
            load_g.wait()
        d_copy(k, 0).wait_recv()
        grad_slab(k, 0)
        x_copy(k, 1).wait_recv()
        d_copy(k, 1).start()
        x_copy(k, 3).wait_recv()
        d_copy(k, 3).start()
        d_copy(k, 1).wait_recv()
        grad_slab(k, 1)
        x_copy(k, 2).wait_recv()
        d_copy(k, 2).start()
        d_copy(k, 3).wait_recv()
        grad_slab(k, 3)
        d_copy(k, 2).wait_recv()
        grad_slab(k, 2)
        z_start(Z_R1, k)

    def reduce_second(k):
        z_arrive(Z_R1, k)
        total = gr[k, :, z, :, high].astype(f32)
        for d in range(1, NZ):
            total += rb1[k, d].astype(f32)
        s1[k] = total.astype(bf16)
        y_start(Y_R1, k)
        for kind, start in ((Y_R0, 0), (Y_R2, NZ // 2)):
            some = pl.ds(start, NZ // 2)
            y_arrive(kind, k)
            total = gr[k, y, some, :, low].astype(f32)
            for d in range(1, NY):
                total += rb0[k, d, some].astype(f32)
            s0[k, some] = total.astype(bf16)
            for to in range(start, start + NZ // 2):

                @pl.when(to != z)
                def _():
                    dst = q0.at[k, lax.rem(to + NZ - z, NZ)]
                    who = (y * NZ + to, tensor)
                    copy(s0.at[k, to], dst, zs.at[Z_R0, k], zr.at[Z_R0, k], who).start()

    def step(k, cols, grad_owned):
        first = beta_one * m1_ref[k, :, cols] + (1.0 - beta_one) * grad_owned
        second = beta_two * m2_ref[k, :, cols] + (1.0 - beta_two) * grad_owned * grad_owned
        nf_ref[k, :, cols] = first
        ns_ref[k, :, cols] = second
        low_step = first / bias_one / (jnp.sqrt(second / bias_two) + adam_eps)
        return low_step.astype(bf16)

    def moments(k):
        if k == 0:
            load_m1.wait()
            load_m2.wait()
        z_arrive(Z_R0, k)
        total = s0[k, z].astype(f32)
        for d in range(1, NZ):
            total += q0[k, d].astype(f32)
        low_step = step(k, low, total)
        for to in range(NY):
            lown[k, to] = low_step[:, to * LANES : (to + 1) * LANES]
        y_start(Y_L0, k)
        la[k, y, z] = lown[k, y]
        y_arrive(Y_R1, k)
        total = s1[k, y].astype(f32)
        for d in range(1, NY):
            total += q1[k, d].astype(f32)
        lb[k, y, z] = step(k, high, total)
        z_start(Z_L1, k)

    def rows_out(k):
        for d in (2, 1, 3):
            p_copy(k, d).start()
        p4[k, :, share, mine] = pg[k, :, z, share]

    def rows_in(k):
        p_all(k).wait_recv()
        e_copy(k).start()

    def spread_second(k):
        y_arrive(Y_L0, k)
        z_start(Z_L0, k)
        z_arrive(Z_L1, k)
        y_start(Y_L1, k)

    def update(k):
        e_copy(k).wait_recv()
        z_arrive(Z_L0, k)
        whole = jnp.dot(
            p4[k].reshape(NY * ROWS, NX * LANES),
            la[k].reshape(NX * LANES, LANES),
            preferred_element_type=f32,
        )
        uq[k] = whole.astype(bf16).reshape(NY, ROWS, LANES)
        y_start(Y_U, k)
        u_ref[k, :, pl.ds(pl.multiple_of(y * LANES, LANES), LANES)] = uq[k, y]

    def finish(k):
        y_arrive(Y_L1, k)
        part = jnp.dot(
            p_ref[k], lb[k].reshape(NX * LANES, LANES), preferred_element_type=f32
        )
        u_ref[k, :, high] = part.astype(bf16)
        y_arrive(Y_U, k)

    load_p.wait()
    pl.semaphore_wait(barrier, NZ - 1 + NY - 1 + NX - 1 + 1)

    for what, k in (
        (gather_first, 0), (gather_first, 1), (gather_second, 0), (gather_first, 2), (gather_second, 1),
        (lower, 0), (gather_second, 2), (lower, 1), (grad, 0), (lower, 2),
        (rows_out, 0), (rows_out, 1), (rows_out, 2),
        (grad, 1), (reduce_second, 0), (grad, 2), (moments, 0), (reduce_second, 1), (spread_second, 0),
        (rows_in, 0), (rows_in, 1), (moments, 1), (reduce_second, 2), (update, 0), (spread_second, 1),
        (rows_in, 2), (moments, 2), (update, 1), (spread_second, 2), (finish, 0), (update, 2), (finish, 1), (finish, 2),
    ):
        what(k)

    for k in range(NK):
        for kind in range(6):
            if kind != Z_P0 or k == NK - 1:
                z_all(kind, k).wait_send()
        for kind in range(8):
            y_all(kind, k).wait_send()
        for sent in (c_all, d_all, x_all, p_all, e_copy):
            sent(k).wait_send()


def on_device(activations, cotangent, projector, first_moment, second_moment):
    vmem = pl.BlockSpec(memory_space=pltpu.VMEM)
    hbm = pl.BlockSpec(memory_space=pltpu.HBM)
    dma = pltpu.SemaphoreType.DMA
    return pl.pallas_call(
        kernel,
        out_shape=(
            jax.ShapeDtypeStruct((NK, OWN, COLS), f32),
            jax.ShapeDtypeStruct((NK, OWN, COLS), f32),
            jax.ShapeDtypeStruct((NK, ROWS, COLS), bf16),
        ),
        in_specs=[hbm] * 5,
        out_specs=(vmem, vmem, vmem),
        scratch_shapes=[
            pltpu.VMEM((NK, ROWS, NX * LANES), bf16),
            pltpu.VMEM((NK, OWN, COLS), f32),
            pltpu.VMEM((NK, OWN, COLS), f32),
            pltpu.VMEM((NK, NY, NZ, ROWS, LANES), bf16),
            pltpu.VMEM((HALF, NY * SLAB), bf16),
            pltpu.VMEM((NK, TOK, COLS), bf16),
            pltpu.VMEM((HALF, LANES), f32),
            pltpu.VMEM((NK, NX, LANES, TOK), bf16),
            pltpu.VMEM((NK, NY, NZ, OWN, COLS), bf16),
            pltpu.VMEM((NK, NY, NZ, OWN, WIDE), bf16),
            pltpu.VMEM((NK, NZ, NY, OWN, COLS - WIDE), bf16),
            pltpu.VMEM((NK, NZ, OWN, WIDE), bf16),
            pltpu.VMEM((NK, NY, OWN, COLS - WIDE), bf16),
            pltpu.VMEM((NK, NZ, OWN, WIDE), bf16),
            pltpu.VMEM((NK, NY, OWN, COLS - WIDE), bf16),
            pltpu.VMEM((NK, NY, OWN, LANES), bf16),
            pltpu.VMEM((NK, NY, NZ, OWN, LANES), bf16),
            pltpu.VMEM((NK, NY, NZ, OWN, LANES), bf16),
            pltpu.VMEM((NK, NY, ROWS, NX * LANES), bf16),
            pltpu.VMEM((NK, NY, ROWS, LANES), bf16),
            dma((6, NK)), dma((6, NK)), dma((NK, NZ)),
            dma((8, NK)), dma((8, NK)), dma((NK, NY)),
            dma((NK,)), dma((NK, NY + 1)),
            dma((NK,)), dma((NK, NX)),
            dma((NK,)), dma((NK, NX)),
            dma((NK,)), dma((NK,)),
            dma((NK,)), dma((NK,)),
            dma((5,)),
        ],
        compiler_params=pltpu.CompilerParams(
            collective_id=0, has_side_effects=True, vmem_limit_bytes=52 * 2**20
        ),
        name="galore_step",
    )(projector, first_moment, second_moment, activations, cotangent)


def solution(mesh):
    placed = (
        P("dp", None),
        P(None, "dp", "tensor"),
        P(None, "dp", None),
        P(None, "dp", "tensor"),
        P(None, "dp", "tensor"),
    )
    return jax.shard_map(
        on_device,
        mesh=mesh,
        in_specs=placed,
        out_specs=(P(None, "dp", "tensor"), P(None, "dp", "tensor"), P(None, "dp", "tensor")),
        check_vma=False,
    )
```

```python
import jax
import jax.numpy as jnp
from jax import lax
from jax.experimental import pallas as pl
from jax.experimental.pallas import tpu as pltpu
from jax.sharding import PartitionSpec as P

beta_one = 0.9
beta_two = 0.95
adam_eps = 1e-08
bias_one = 1.0 - 0.9**10
bias_two = 1.0 - 0.95**10

MESH = pl.DeviceIdType.MESH
f32, bf16 = jnp.float32, jnp.bfloat16
NK, NY, NZ, NX = 3, 4, 8, 4
TOK, HALF = 768, 384
ROWS, SHARE = 160, 80
BIG, SMALL = 64, 16
SLAB = NZ * ROWS
LANES = 128
COLS, WIDE = 640, 512
OWN = 16

Z_ORDER = (1, 7, 2, 6, 3, 5, 4)
Z_COME = (1, 7, 2, 6, 3, 5, 4)
Z_P0, Z_P1, Z_R0, Z_R1, Z_L0, Z_L1 = range(6)
Y_P0, Y_P1, Y_R0, Y_R1, Y_L0, Y_L1, Y_R2, Y_U = range(8)


def kernel(
    p_hbm, m1_hbm, m2_hbm, a_hbm, g_hbm,
    nf_ref, ns_ref, u_ref,
    p_ref, m1_ref, m2_ref, pg, av, gv, acc, lt, gr, rb0, rb1, s0, s1, q0, q1, lown, la, lb, p4, uq,
    zs, zr, zpr, ys, yr, ypr, cs, cr, xs, xr, ds, dr, ps, pr, es, er, lsem,
):
    dp, tensor = lax.axis_index("dp"), lax.axis_index("tensor")
    y, z, x, c = dp // NZ, dp % NZ, tensor // 2, tensor % 2

    load_a = pltpu.make_async_copy(
        a_hbm.at[pl.ds(pl.multiple_of(c * HALF, HALF), HALF)], av, lsem.at[0]
    )
    load_g = pltpu.make_async_copy(g_hbm, gv, lsem.at[1])
    load_p = pltpu.make_async_copy(p_hbm, p_ref, lsem.at[2])
    load_m1 = pltpu.make_async_copy(m1_hbm, m1_ref, lsem.at[3])
    load_m2 = pltpu.make_async_copy(m2_hbm, m2_ref, lsem.at[4])
    load_p.start()

    zt = [lax.rem(z + d, NZ) for d in range(NZ)]
    yt = [lax.rem(y + d, NY) for d in range(NY)]
    xt = [lax.rem(x + d, NX) for d in range(NX)]
    at_z = [(y * NZ + zt[d], tensor) for d in range(NZ)]
    at_y = [(yt[d] * NZ + z, tensor) for d in range(NY)]
    at_x = [(dp, xt[d] * 2 + c) for d in range(NX)]
    partner = (dp, x * 2 + (1 - c))

    barrier = pltpu.get_barrier_semaphore()

    def greet(who):
        pl.semaphore_signal(barrier, inc=1, device_id=who, device_id_type=MESH)

    for d in range(1, NZ):
        greet(at_z[d])
    for d in range(1, NY):
        greet(at_y[d])
    for d in range(1, NX):
        greet(at_x[d])
    greet(partner)
    load_a.start()
    load_g.start()
    load_m1.start()
    load_m2.start()

    rows0 = pl.ds(pl.multiple_of(c * SHARE, 16), BIG)
    rows1 = pl.ds(pl.multiple_of(c * SHARE + BIG, 16), SMALL)
    share = pl.ds(pl.multiple_of(c * SHARE, 16), SHARE)
    mine = pl.ds(pl.multiple_of(x * LANES, LANES), LANES)
    toks = pl.ds(pl.multiple_of(c * HALF, HALF), HALF)
    low, high = pl.ds(0, WIDE), pl.ds(WIDE, COLS - WIDE)

    def copy(src, dst, send, recv, who):
        return pltpu.make_async_remote_copy(
            src_ref=src, dst_ref=dst, send_sem=send, recv_sem=recv,
            device_id=who, device_id_type=MESH,
        )

    def z_copy(kind, k, d):
        to = zt[d]
        if kind == Z_P0:
            src, dst = p_hbm.at[k, rows0, mine], pg.at[k, y, z, rows0]
        elif kind == Z_P1:
            src = dst = pg.at[k, :, z, rows1]
        elif kind == Z_R1:
            src, dst = gr.at[k, :, to, :, high], rb1.at[k, d]
        elif kind == Z_L0:
            src = dst = la.at[k, :, z]
        else:
            src = dst = lb.at[k, y, z]
        recv = zpr.at[k, d] if kind == Z_P0 else zr.at[kind, k]
        return copy(src, dst, zs.at[kind, k], recv, at_z[d])

    def y_copy(kind, k, d):
        to = yt[d]
        if kind == Y_P1:
            src, dst = p_hbm.at[k, rows1, mine], pg.at[k, y, z, rows1]
        elif kind == Y_R1:
            src, dst = s1.at[k, to], q1.at[k, d]
        elif kind == Y_L0:
            src, dst = lown.at[k, to], la.at[k, y, z]
        elif kind == Y_L1:
            src = dst = lb.at[k, y]
        else:
            quarter = pl.ds(pl.multiple_of(y * LANES, LANES), LANES)
            src, dst = uq.at[k, to], u_ref.at[k, :, quarter]
        return copy(src, dst, ys.at[kind, k], yr.at[kind, k], at_y[d])

    def y_block(k, at):
        here = pg.at[k, y, at, rows0]
        for d in (2, 1, 3):
            copy(here, here, ys.at[Y_P0, k], ypr.at[k, d], at_y[d]).start()

    def y_slab(k, d):
        here = pg.at[k, yt[(NY - d) % NY], :, rows0]
        return copy(here, here, ys.at[Y_P0, k], ypr.at[k, d], partner)

    def c_copy(k, i):
        here = pg.at[k, :, :, rows1] if i == NY else pg.at[k, yt[(NY - i) % NY], :, rows0]
        return copy(here, here, cs.at[k], cr.at[k, i], partner)

    def x_copy(k, d):
        here = lt.at[k, x, :, toks]
        return copy(here, here, xs.at[k], xr.at[k, d], at_x[d])

    def d_copy(k, d):
        here = lt.at[k, xt[(NX - d) % NX], :, toks]
        return copy(here, here, ds.at[k], dr.at[k, d], partner)

    def p_copy(k, d):
        return copy(pg.at[k, :, z, share], p4.at[k, :, share, mine], ps.at[k], pr.at[k], at_x[d])

    def e_copy(k):
        here = p4.at[k, :, share]
        return copy(here, here, es.at[k], er.at[k], partner)

    def z_all(kind, k):
        some = pl.ds(1, NZ - 1)
        whole = {
            Z_P0: pg.at[k, 0, some, pl.ds(0, BIG)],
            Z_P1: pg.at[k, :, some, rows1],
            Z_R0: q0.at[k, some],
            Z_R1: rb1.at[k, some],
            Z_L0: la.at[k, :, some],
            Z_L1: lb.at[k, y, some],
        }[kind]
        return copy(whole, whole, zs.at[kind, k], zr.at[kind, k], partner)

    def y_all(kind, k):
        some = pl.ds(1, NY - 1)
        whole = {
            Y_P0: pg.at[k, some, :, pl.ds(0, BIG)],
            Y_P1: pg.at[k, some, z, rows1],
            Y_R0: rb0.at[k, some, pl.ds(0, NZ // 2)],
            Y_R2: rb0.at[k, some, pl.ds(NZ // 2, NZ // 2)],
            Y_R1: q1.at[k, some],
            Y_L0: la.at[k, some, z],
            Y_L1: lb.at[k, some],
            Y_U: uq.at[k, some],
        }[kind]
        return copy(whole, whole, ys.at[kind, k], yr.at[kind, k], partner)

    def x_all(k):
        whole = lt.at[k, pl.ds(1, NX - 1), :, pl.ds(0, HALF)]
        return copy(whole, whole, xs.at[k], xr.at[k, 0], partner)

    def p_all(k):
        whole = pg.at[k, :, pl.ds(1, NX - 1), pl.ds(0, SHARE)]
        return copy(whole, whole, ps.at[k], pr.at[k], partner)

    def c_all(k):
        whole = pg.at[k, :, :, pl.ds(0, SHARE)]
        return copy(whole, whole, cs.at[k], cr.at[k, 0], partner)

    def d_all(k):
        whole = lt.at[k, :, :, pl.ds(0, HALF)]
        return copy(whole, whole, ds.at[k], dr.at[k, 0], partner)

    def z_start(kind, k):
        for d in Z_ORDER:
            z_copy(kind, k, d).start()

    def z_arrive(kind, k):
        z_all(kind, k).wait_recv()

    def y_start(kind, k):
        for d in (2, 1, 3):
            y_copy(kind, k, d).start()

    def y_arrive(kind, k):
        y_all(kind, k).wait_recv()

    def gather_first(k):
        if k:
            z_all(Z_P0, k - 1).wait_send()
        z_start(Z_P0, k)
        y_start(Y_P1, k)
        if k == 0:
            load_p.wait()
        pg[k, y, z, share] = p_ref[k, share, mine]
        y_block(k, z)

    def gather_second(k):
        y_arrive(Y_P1, k)
        z_start(Z_P1, k)
        for d in Z_COME:
            z_copy(Z_P0, k, d).wait_recv()
            y_block(k, zt[NZ - d])
        c_copy(k, 0).start()

    def add_slab(k, d, first=False):
        at = yt[(NY - d) % NY]
        part = jnp.dot(
            av[:, pl.ds(pl.multiple_of(at * SLAB, LANES), SLAB)],
            pg[k, at].reshape(SLAB, LANES),
            preferred_element_type=f32,
        )
        acc[...] = part if first else acc[...] + part

    def lower(k):
        z_arrive(Z_P1, k)
        c_copy(k, NY).start()
        if k == 0:
            load_a.wait()
        y_slab(k, 1).wait_recv()
        c_copy(k, 1).start()
        y_slab(k, 3).wait_recv()
        c_copy(k, 3).start()
        y_slab(k, 2).wait_recv()
        c_copy(k, 2).start()
        c_copy(k, NY).wait_recv()
        c_copy(k, 0).wait_recv()
        add_slab(k, 0, True)
        c_copy(k, 1).wait_recv()
        add_slab(k, 1)
        c_copy(k, 3).wait_recv()
        add_slab(k, 3)
        c_copy(k, 2).wait_recv()
        add_slab(k, 2)
        lt[k, x, :, toks] = acc[...].T.astype(bf16)
        for d in (2, 1, 3):
            x_copy(k, d).start()
        d_copy(k, 0).start()

    def grad_slab(k, d):
        at = xt[(NX - d) % NX]
        part = jnp.dot(lt[k, at], gv[k], preferred_element_type=f32)
        gr[k, at] = part.astype(bf16).reshape(NZ, OWN, COLS)

        @pl.when(at != y)
        def _():
            d = lax.rem(at + NY - y, NY)
            for kind, some in ((Y_R0, pl.ds(0, NZ // 2)), (Y_R2, pl.ds(NZ // 2, NZ // 2))):
                src, dst = gr.at[k, at, some, :, low], rb0.at[k, d, some]
                copy(src, dst, ys.at[kind, k], yr.at[kind, k], (at * NZ + z, tensor)).start()

    def grad(k):
        if k == 0:
            load_g.wait()
        d_copy(k, 0).wait_recv()
        grad_slab(k, 0)
        x_copy(k, 1).wait_recv()
        d_copy(k, 1).start()
        x_copy(k, 3).wait_recv()
        d_copy(k, 3).start()
        d_copy(k, 1).wait_recv()
        grad_slab(k, 1)
        x_copy(k, 2).wait_recv()
        d_copy(k, 2).start()
        d_copy(k, 3).wait_recv()
        grad_slab(k, 3)
        d_copy(k, 2).wait_recv()
        grad_slab(k, 2)
        z_start(Z_R1, k)

    def reduce_second(k):
        z_arrive(Z_R1, k)
        total = gr[k, :, z, :, high].astype(f32)
        for d in range(1, NZ):
            total += rb1[k, d].astype(f32)
        s1[k] = total.astype(bf16)
        y_start(Y_R1, k)
        for kind, start in ((Y_R0, 0), (Y_R2, NZ // 2)):
            some = pl.ds(start, NZ // 2)
            y_arrive(kind, k)
            total = gr[k, y, some, :, low].astype(f32)
            for d in range(1, NY):
                total += rb0[k, d, some].astype(f32)
            s0[k, some] = total.astype(bf16)
            for to in range(start, start + NZ // 2):

                @pl.when(to != z)
                def _():
                    dst = q0.at[k, lax.rem(to + NZ - z, NZ)]
                    who = (y * NZ + to, tensor)
                    copy(s0.at[k, to], dst, zs.at[Z_R0, k], zr.at[Z_R0, k], who).start()

    def step(k, cols, grad_owned):
        first = beta_one * m1_ref[k, :, cols] + (1.0 - beta_one) * grad_owned
        second = beta_two * m2_ref[k, :, cols] + (1.0 - beta_two) * grad_owned * grad_owned
        nf_ref[k, :, cols] = first
        ns_ref[k, :, cols] = second
        low_step = first / bias_one / (jnp.sqrt(second / bias_two) + adam_eps)
        return low_step.astype(bf16)

    def moments(k):
        if k == 0:
            load_m1.wait()
            load_m2.wait()
        z_arrive(Z_R0, k)
        total = s0[k, z].astype(f32)
        for d in range(1, NZ):
            total += q0[k, d].astype(f32)
        low_step = step(k, low, total)
        for to in range(NY):
            lown[k, to] = low_step[:, to * LANES : (to + 1) * LANES]
        y_start(Y_L0, k)
        la[k, y, z] = lown[k, y]
        y_arrive(Y_R1, k)
        total = s1[k, y].astype(f32)
        for d in range(1, NY):
            total += q1[k, d].astype(f32)
        lb[k, y, z] = step(k, high, total)
        z_start(Z_L1, k)

    def rows_out(k):
        for d in (2, 1, 3):
            p_copy(k, d).start()
        p4[k, :, share, mine] = pg[k, :, z, share]

    def rows_in(k):
        p_all(k).wait_recv()
        e_copy(k).start()

    def spread_second(k):
        y_arrive(Y_L0, k)
        z_start(Z_L0, k)
        z_arrive(Z_L1, k)
        y_start(Y_L1, k)

    def update(k):
        e_copy(k).wait_recv()
        z_arrive(Z_L0, k)
        whole = jnp.dot(
            p4[k].reshape(NY * ROWS, NX * LANES),
            la[k].reshape(NX * LANES, LANES),
            preferred_element_type=f32,
        )
        uq[k] = whole.astype(bf16).reshape(NY, ROWS, LANES)
        y_start(Y_U, k)
        u_ref[k, :, pl.ds(pl.multiple_of(y * LANES, LANES), LANES)] = uq[k, y]

    def finish(k):
        y_arrive(Y_L1, k)
        part = jnp.dot(
            p_ref[k], lb[k].reshape(NX * LANES, LANES), preferred_element_type=f32
        )
        u_ref[k, :, high] = part.astype(bf16)
        y_arrive(Y_U, k)

    pl.semaphore_wait(barrier, NZ - 1 + NY - 1 + NX - 1 + 1)

    for what, k in (
        (gather_first, 0), (gather_first, 1), (gather_second, 0), (gather_first, 2), (gather_second, 1),
        (lower, 0), (gather_second, 2), (lower, 1), (grad, 0), (lower, 2),
        (grad, 1), (reduce_second, 0), (grad, 2), (rows_out, 0), (rows_out, 1),
        (rows_out, 2), (moments, 0), (reduce_second, 1), (spread_second, 0), (moments, 1),
        (rows_in, 0), (rows_in, 1), (reduce_second, 2), (spread_second, 1), (update, 0),
        (rows_in, 2), (moments, 2), (update, 1), (spread_second, 2), (update, 2),
        (finish, 0), (finish, 1), (finish, 2),
    ):
        what(k)

    for k in range(NK):
        for kind in range(6):
            if kind != Z_P0 or k == NK - 1:
                z_all(kind, k).wait_send()
        for kind in range(8):
            y_all(kind, k).wait_send()
        for sent in (c_all, d_all, x_all, p_all, e_copy):
            sent(k).wait_send()


def place(nf, ns, u, nf_out, ns_out, u_out, sem):
    copies = [
        pltpu.make_async_copy(src, dst, sem.at[i])
        for i, (src, dst) in enumerate(((u, u_out), (nf, nf_out), (ns, ns_out)))
    ]
    for one in copies:
        one.start()
    for one in copies:
        one.wait()


def on_device(activations, cotangent, projector, first_moment, second_moment):
    vmem = pl.BlockSpec(memory_space=pltpu.VMEM)
    hbm = pl.BlockSpec(memory_space=pltpu.HBM)
    dma = pltpu.SemaphoreType.DMA
    shapes = (
        jax.ShapeDtypeStruct((NK, OWN, COLS), f32),
        jax.ShapeDtypeStruct((NK, OWN, COLS), f32),
        jax.ShapeDtypeStruct((NK, ROWS, COLS), bf16),
    )
    results = pl.pallas_call(
        kernel,
        out_shape=shapes,
        in_specs=[hbm] * 5,
        out_specs=(vmem, vmem, vmem),
        scratch_shapes=[
            pltpu.VMEM((NK, ROWS, NX * LANES), bf16),
            pltpu.VMEM((NK, OWN, COLS), f32),
            pltpu.VMEM((NK, OWN, COLS), f32),
            pltpu.VMEM((NK, NY, NZ, ROWS, LANES), bf16),
            pltpu.VMEM((HALF, NY * SLAB), bf16),
            pltpu.VMEM((NK, TOK, COLS), bf16),
            pltpu.VMEM((HALF, LANES), f32),
            pltpu.VMEM((NK, NX, LANES, TOK), bf16),
            pltpu.VMEM((NK, NY, NZ, OWN, COLS), bf16),
            pltpu.VMEM((NK, NY, NZ, OWN, WIDE), bf16),
            pltpu.VMEM((NK, NZ, NY, OWN, COLS - WIDE), bf16),
            pltpu.VMEM((NK, NZ, OWN, WIDE), bf16),
            pltpu.VMEM((NK, NY, OWN, COLS - WIDE), bf16),
            pltpu.VMEM((NK, NZ, OWN, WIDE), bf16),
            pltpu.VMEM((NK, NY, OWN, COLS - WIDE), bf16),
            pltpu.VMEM((NK, NY, OWN, LANES), bf16),
            pltpu.VMEM((NK, NY, NZ, OWN, LANES), bf16),
            pltpu.VMEM((NK, NY, NZ, OWN, LANES), bf16),
            pltpu.VMEM((NK, NY, ROWS, NX * LANES), bf16),
            pltpu.VMEM((NK, NY, ROWS, LANES), bf16),
            dma((6, NK)), dma((6, NK)), dma((NK, NZ)),
            dma((8, NK)), dma((8, NK)), dma((NK, NY)),
            dma((NK,)), dma((NK, NY + 1)),
            dma((NK,)), dma((NK, NX)),
            dma((NK,)), dma((NK, NX)),
            dma((NK,)), dma((NK,)),
            dma((NK,)), dma((NK,)),
            dma((5,)),
        ],
        compiler_params=pltpu.CompilerParams(
            collective_id=0, has_side_effects=True, vmem_limit_bytes=52 * 2**20
        ),
        name="galore_step",
    )(projector, first_moment, second_moment, activations, cotangent)
    return pl.pallas_call(
        place,
        out_shape=shapes,
        in_specs=[pl.BlockSpec(memory_space=pl.ANY)] * 3,
        out_specs=(hbm,) * 3,
        scratch_shapes=[dma((3,))],
        compiler_params=pltpu.CompilerParams(vmem_limit_bytes=16 * 2**20),
        name="place_results",
    )(*results)


def solution(mesh):
    placed = (
        P("dp", None),
        P(None, "dp", "tensor"),
        P(None, "dp", None),
        P(None, "dp", "tensor"),
        P(None, "dp", "tensor"),
    )
    return jax.shard_map(
        on_device,
        mesh=mesh,
        in_specs=placed,
        out_specs=(P(None, "dp", "tensor"), P(None, "dp", "tensor"), P(None, "dp", "tensor")),
        check_vma=False,
    )
```

```python
import jax
import jax.numpy as jnp
from jax import lax
from jax.experimental import pallas as pl
from jax.experimental.pallas import tpu as pltpu
from jax.sharding import PartitionSpec as P

beta_one = 0.9
beta_two = 0.95
adam_eps = 1e-08
bias_one = 1.0 - 0.9**10
bias_two = 1.0 - 0.95**10

MESH = pl.DeviceIdType.MESH
f32, bf16 = jnp.float32, jnp.bfloat16
NK, NY, NZ, NX = 3, 4, 8, 4
TOK, HALF = 768, 384
ROWS, SHARE = 160, 80
BIG, SMALL = 64, 16
SLAB = NZ * ROWS
LANES = 128
COLS, WIDE = 640, 512
OWN = 16

Z_ORDER = (1, 7, 2, 6, 3, 5, 4)
Z_COME = (1, 7, 2, 6, 3, 5, 4)
Z_P0, Z_P1, Z_R0, Z_R1, Z_L0, Z_L1 = range(6)
Y_P0, Y_P1, Y_R0, Y_R1, Y_L0, Y_L1, Y_R2, Y_U = range(8)


def kernel(
    p_hbm, m1_hbm, m2_hbm, a_hbm, g_hbm,
    nf_ref, ns_ref, u_ref,
    p_ref, m1_ref, m2_ref, pg, av, gv, acc, lt, gr, rb0, rb1, s0, s1, q0, q1, lown, la, lb, p4, uq,
    zs, zr, zpr, ys, yr, ypr, cs, cr, xs, xr, ds, dr, ps, pr, es, er, lsem,
):
    dp, tensor = lax.axis_index("dp"), lax.axis_index("tensor")
    y, z, x, c = dp // NZ, dp % NZ, tensor // 2, tensor % 2

    load_a = pltpu.make_async_copy(
        a_hbm.at[pl.ds(pl.multiple_of(c * HALF, HALF), HALF)], av, lsem.at[0]
    )
    load_g = pltpu.make_async_copy(g_hbm, gv, lsem.at[1])
    load_p = pltpu.make_async_copy(p_hbm, p_ref, lsem.at[2])
    load_m1 = pltpu.make_async_copy(m1_hbm, m1_ref, lsem.at[3])
    load_m2 = pltpu.make_async_copy(m2_hbm, m2_ref, lsem.at[4])
    load_p.start()

    zt = [lax.rem(z + d, NZ) for d in range(NZ)]
    yt = [lax.rem(y + d, NY) for d in range(NY)]
    xt = [lax.rem(x + d, NX) for d in range(NX)]
    at_z = [(y * NZ + zt[d], tensor) for d in range(NZ)]
    at_y = [(yt[d] * NZ + z, tensor) for d in range(NY)]
    at_x = [(dp, xt[d] * 2 + c) for d in range(NX)]
    partner = (dp, x * 2 + (1 - c))

    barrier = pltpu.get_barrier_semaphore()

    def greet(who):
        pl.semaphore_signal(barrier, inc=1, device_id=who, device_id_type=MESH)

    for d in range(1, NZ):
        greet(at_z[d])
    for d in range(1, NY):
        greet(at_y[d])
    for d in range(1, NX):
        greet(at_x[d])
    greet(partner)
    load_a.start()
    load_g.start()
    load_m1.start()
    load_m2.start()

    rows0 = pl.ds(pl.multiple_of(c * SHARE, 16), BIG)
    rows1 = pl.ds(pl.multiple_of(c * SHARE + BIG, 16), SMALL)
    share = pl.ds(pl.multiple_of(c * SHARE, 16), SHARE)
    mine = pl.ds(pl.multiple_of(x * LANES, LANES), LANES)
    toks = pl.ds(pl.multiple_of(c * HALF, HALF), HALF)
    low, high = pl.ds(0, WIDE), pl.ds(WIDE, COLS - WIDE)

    def copy(src, dst, send, recv, who):
        return pltpu.make_async_remote_copy(
            src_ref=src, dst_ref=dst, send_sem=send, recv_sem=recv,
            device_id=who, device_id_type=MESH,
        )

    def z_copy(kind, k, d):
        to = zt[d]
        if kind == Z_P0:
            src, dst = p_hbm.at[k, rows0, mine], pg.at[k, y, z, rows0]
        elif kind == Z_P1:
            src = dst = pg.at[k, :, z, rows1]
        elif kind == Z_R1:
            src, dst = gr.at[k, :, to, :, high], rb1.at[k, d]
        elif kind == Z_L0:
            src = dst = la.at[k, :, z]
        else:
            src = dst = lb.at[k, y, z]
        recv = zpr.at[k, d] if kind == Z_P0 else zr.at[kind, k]
        return copy(src, dst, zs.at[kind, k], recv, at_z[d])

    def y_copy(kind, k, d):
        to = yt[d]
        if kind == Y_P1:
            src, dst = p_hbm.at[k, rows1, mine], pg.at[k, y, z, rows1]
        elif kind == Y_R1:
            src, dst = s1.at[k, to], q1.at[k, d]
        elif kind == Y_L0:
            src, dst = lown.at[k, to], la.at[k, y, z]
        elif kind == Y_L1:
            src = dst = lb.at[k, y]
        else:
            quarter = pl.ds(pl.multiple_of(y * LANES, LANES), LANES)
            src, dst = uq.at[k, to], u_ref.at[k, :, quarter]
        return copy(src, dst, ys.at[kind, k], yr.at[kind, k], at_y[d])

    def y_block(k, at):
        here = pg.at[k, y, at, rows0]
        for d in (2, 1, 3):
            copy(here, here, ys.at[Y_P0, k], ypr.at[k, d], at_y[d]).start()

    def y_slab(k, d):
        here = pg.at[k, yt[(NY - d) % NY], :, rows0]
        return copy(here, here, ys.at[Y_P0, k], ypr.at[k, d], partner)

    def c_copy(k, i):
        here = pg.at[k, :, :, rows1] if i == NY else pg.at[k, yt[(NY - i) % NY], :, rows0]
        return copy(here, here, cs.at[k], cr.at[k, i], partner)

    def x_copy(k, d):
        here = lt.at[k, x, :, toks]
        return copy(here, here, xs.at[k], xr.at[k, d], at_x[d])

    def d_copy(k, d):
        here = lt.at[k, xt[(NX - d) % NX], :, toks]
        return copy(here, here, ds.at[k], dr.at[k, d], partner)

    def p_copy(k, d):
        return copy(pg.at[k, :, z, share], p4.at[k, :, share, mine], ps.at[k], pr.at[k], at_x[d])

    def e_copy(k):
        here = p4.at[k, :, share]
        return copy(here, here, es.at[k], er.at[k], partner)

    def z_all(kind, k):
        some = pl.ds(1, NZ - 1)
        whole = {
            Z_P0: pg.at[k, 0, some, pl.ds(0, BIG)],
            Z_P1: pg.at[k, :, some, rows1],
            Z_R0: q0.at[k, some],
            Z_R1: rb1.at[k, some],
            Z_L0: la.at[k, :, some],
            Z_L1: lb.at[k, y, some],
        }[kind]
        return copy(whole, whole, zs.at[kind, k], zr.at[kind, k], partner)

    def y_all(kind, k):
        some = pl.ds(1, NY - 1)
        whole = {
            Y_P0: pg.at[k, some, :, pl.ds(0, BIG)],
            Y_P1: pg.at[k, some, z, rows1],
            Y_R0: rb0.at[k, some, pl.ds(0, NZ // 2)],
            Y_R2: rb0.at[k, some, pl.ds(NZ // 2, NZ // 2)],
            Y_R1: q1.at[k, some],
            Y_L0: la.at[k, some, z],
            Y_L1: lb.at[k, some],
            Y_U: uq.at[k, some],
        }[kind]
        return copy(whole, whole, ys.at[kind, k], yr.at[kind, k], partner)

    def x_all(k):
        whole = lt.at[k, pl.ds(1, NX - 1), :, pl.ds(0, HALF)]
        return copy(whole, whole, xs.at[k], xr.at[k, 0], partner)

    def p_all(k):
        whole = pg.at[k, :, pl.ds(1, NX - 1), pl.ds(0, SHARE)]
        return copy(whole, whole, ps.at[k], pr.at[k], partner)

    def c_all(k):
        whole = pg.at[k, :, :, pl.ds(0, SHARE)]
        return copy(whole, whole, cs.at[k], cr.at[k, 0], partner)

    def d_all(k):
        whole = lt.at[k, :, :, pl.ds(0, HALF)]
        return copy(whole, whole, ds.at[k], dr.at[k, 0], partner)

    def z_start(kind, k):
        for d in Z_ORDER:
            z_copy(kind, k, d).start()

    def z_arrive(kind, k):
        z_all(kind, k).wait_recv()

    def y_start(kind, k):
        for d in (2, 1, 3):
            y_copy(kind, k, d).start()

    def y_arrive(kind, k):
        y_all(kind, k).wait_recv()

    def gather_first(k):
        if k:
            z_all(Z_P0, k - 1).wait_send()
        z_start(Z_P0, k)
        y_start(Y_P1, k)
        if k == 0:
            load_p.wait()
        pg[k, y, z, share] = p_ref[k, share, mine]
        y_block(k, z)

    def gather_second(k):
        y_arrive(Y_P1, k)
        z_start(Z_P1, k)
        for d in Z_COME:
            z_copy(Z_P0, k, d).wait_recv()
            y_block(k, zt[NZ - d])
        c_copy(k, 0).start()

    def add_slab(k, d, first=False):
        at = yt[(NY - d) % NY]
        part = jnp.dot(
            av[:, pl.ds(pl.multiple_of(at * SLAB, LANES), SLAB)],
            pg[k, at].reshape(SLAB, LANES),
            preferred_element_type=f32,
        )
        acc[...] = part if first else acc[...] + part

    def lower(k):
        z_arrive(Z_P1, k)
        c_copy(k, NY).start()
        if k == 0:
            load_a.wait()
        y_slab(k, 1).wait_recv()
        c_copy(k, 1).start()
        y_slab(k, 3).wait_recv()
        c_copy(k, 3).start()
        y_slab(k, 2).wait_recv()
        c_copy(k, 2).start()
        c_copy(k, NY).wait_recv()
        c_copy(k, 0).wait_recv()
        add_slab(k, 0, True)
        c_copy(k, 1).wait_recv()
        add_slab(k, 1)
        c_copy(k, 3).wait_recv()
        add_slab(k, 3)
        c_copy(k, 2).wait_recv()
        add_slab(k, 2)
        lt[k, x, :, toks] = acc[...].T.astype(bf16)
        for d in (2, 1, 3):
            x_copy(k, d).start()
        d_copy(k, 0).start()

    def grad_slab(k, d):
        at = xt[(NX - d) % NX]
        part = jnp.dot(lt[k, at], gv[k], preferred_element_type=f32)
        gr[k, at] = part.astype(bf16).reshape(NZ, OWN, COLS)

        @pl.when(at != y)
        def _():
            d = lax.rem(at + NY - y, NY)
            for kind, some in ((Y_R0, pl.ds(0, NZ // 2)), (Y_R2, pl.ds(NZ // 2, NZ // 2))):
                src, dst = gr.at[k, at, some, :, low], rb0.at[k, d, some]
                copy(src, dst, ys.at[kind, k], yr.at[kind, k], (at * NZ + z, tensor)).start()

    def grad(k):
        if k == 0:
            load_g.wait()
        for d in (1, 3, 2):
            x_copy(k, d).wait_recv()
            d_copy(k, d).start()
        for d in (0, 1, 3, 2):
            d_copy(k, d).wait_recv()
            grad_slab(k, d)
        z_start(Z_R1, k)

    def reduce_second(k):
        z_arrive(Z_R1, k)
        total = gr[k, :, z, :, high].astype(f32)
        for d in range(1, NZ):
            total += rb1[k, d].astype(f32)
        s1[k] = total.astype(bf16)
        y_start(Y_R1, k)
        for kind, start in ((Y_R0, 0), (Y_R2, NZ // 2)):
            some = pl.ds(start, NZ // 2)
            y_arrive(kind, k)
            total = gr[k, y, some, :, low].astype(f32)
            for d in range(1, NY):
                total += rb0[k, d, some].astype(f32)
            s0[k, some] = total.astype(bf16)
            for to in range(start, start + NZ // 2):

                @pl.when(to != z)
                def _():
                    dst = q0.at[k, lax.rem(to + NZ - z, NZ)]
                    who = (y * NZ + to, tensor)
                    copy(s0.at[k, to], dst, zs.at[Z_R0, k], zr.at[Z_R0, k], who).start()

    def step(k, cols, grad_owned):
        first = beta_one * m1_ref[k, :, cols] + (1.0 - beta_one) * grad_owned
        second = beta_two * m2_ref[k, :, cols] + (1.0 - beta_two) * grad_owned * grad_owned
        nf_ref[k, :, cols] = first
        ns_ref[k, :, cols] = second
        low_step = first / bias_one / (jnp.sqrt(second / bias_two) + adam_eps)
        return low_step.astype(bf16)

    def moments(k):
        if k == 0:
            load_m1.wait()
            load_m2.wait()
        z_arrive(Z_R0, k)
        total = s0[k, z].astype(f32)
        for d in range(1, NZ):
            total += q0[k, d].astype(f32)
        low_step = step(k, low, total)
        for to in range(NY):
            lown[k, to] = low_step[:, to * LANES : (to + 1) * LANES]
        y_start(Y_L0, k)
        la[k, y, z] = lown[k, y]
        y_arrive(Y_R1, k)
        total = s1[k, y].astype(f32)
        for d in range(1, NY):
            total += q1[k, d].astype(f32)
        lb[k, y, z] = step(k, high, total)
        z_start(Z_L1, k)

    def rows_out(k):
        for d in (2, 1, 3):
            p_copy(k, d).start()
        p4[k, :, share, mine] = pg[k, :, z, share]

    def rows_in(k):
        p_all(k).wait_recv()
        e_copy(k).start()

    def spread_second(k):
        y_arrive(Y_L0, k)
        z_start(Z_L0, k)
        z_arrive(Z_L1, k)
        y_start(Y_L1, k)

    def update(k):
        e_copy(k).wait_recv()
        z_arrive(Z_L0, k)
        whole = jnp.dot(
            p4[k].reshape(NY * ROWS, NX * LANES),
            la[k].reshape(NX * LANES, LANES),
            preferred_element_type=f32,
        )
        uq[k] = whole.astype(bf16).reshape(NY, ROWS, LANES)
        y_start(Y_U, k)
        u_ref[k, :, pl.ds(pl.multiple_of(y * LANES, LANES), LANES)] = uq[k, y]

    def finish(k):
        y_arrive(Y_L1, k)
        part = jnp.dot(
            p_ref[k], lb[k].reshape(NX * LANES, LANES), preferred_element_type=f32
        )
        u_ref[k, :, high] = part.astype(bf16)
        y_arrive(Y_U, k)

    pl.semaphore_wait(barrier, NZ - 1 + NY - 1 + NX - 1 + 1)

    for what, k in (
        (gather_first, 0), (gather_first, 1), (gather_second, 0), (gather_first, 2), (gather_second, 1),
        (lower, 0), (gather_second, 2), (lower, 1), (grad, 0), (lower, 2),
        (grad, 1), (reduce_second, 0), (grad, 2), (rows_out, 0), (rows_out, 1),
        (rows_out, 2), (moments, 0), (reduce_second, 1), (spread_second, 0), (moments, 1),
        (rows_in, 0), (rows_in, 1), (reduce_second, 2), (spread_second, 1), (update, 0),
        (rows_in, 2), (moments, 2), (update, 1), (spread_second, 2), (update, 2),
        (finish, 0), (finish, 1), (finish, 2),
    ):
        what(k)

    for k in range(NK):
        for kind in range(6):
            if kind != Z_P0 or k == NK - 1:
                z_all(kind, k).wait_send()
        for kind in range(8):
            y_all(kind, k).wait_send()
        for sent in (c_all, d_all, x_all, p_all, e_copy):
            sent(k).wait_send()


def place(nf, ns, u, nf_out, ns_out, u_out, sem):
    copies = [
        pltpu.make_async_copy(src, dst, sem.at[i])
        for i, (src, dst) in enumerate(((u, u_out), (nf, nf_out), (ns, ns_out)))
    ]
    for one in copies:
        one.start()
    for one in copies:
        one.wait()


def on_device(activations, cotangent, projector, first_moment, second_moment):
    vmem = pl.BlockSpec(memory_space=pltpu.VMEM)
    hbm = pl.BlockSpec(memory_space=pltpu.HBM)
    dma = pltpu.SemaphoreType.DMA
    shapes = (
        jax.ShapeDtypeStruct((NK, OWN, COLS), f32),
        jax.ShapeDtypeStruct((NK, OWN, COLS), f32),
        jax.ShapeDtypeStruct((NK, ROWS, COLS), bf16),
    )
    results = pl.pallas_call(
        kernel,
        out_shape=shapes,
        in_specs=[hbm] * 5,
        out_specs=(vmem, vmem, vmem),
        scratch_shapes=[
            pltpu.VMEM((NK, ROWS, NX * LANES), bf16),
            pltpu.VMEM((NK, OWN, COLS), f32),
            pltpu.VMEM((NK, OWN, COLS), f32),
            pltpu.VMEM((NK, NY, NZ, ROWS, LANES), bf16),
            pltpu.VMEM((HALF, NY * SLAB), bf16),
            pltpu.VMEM((NK, TOK, COLS), bf16),
            pltpu.VMEM((HALF, LANES), f32),
            pltpu.VMEM((NK, NX, LANES, TOK), bf16),
            pltpu.VMEM((NK, NY, NZ, OWN, COLS), bf16),
            pltpu.VMEM((NK, NY, NZ, OWN, WIDE), bf16),
            pltpu.VMEM((NK, NZ, NY, OWN, COLS - WIDE), bf16),
            pltpu.VMEM((NK, NZ, OWN, WIDE), bf16),
            pltpu.VMEM((NK, NY, OWN, COLS - WIDE), bf16),
            pltpu.VMEM((NK, NZ, OWN, WIDE), bf16),
            pltpu.VMEM((NK, NY, OWN, COLS - WIDE), bf16),
            pltpu.VMEM((NK, NY, OWN, LANES), bf16),
            pltpu.VMEM((NK, NY, NZ, OWN, LANES), bf16),
            pltpu.VMEM((NK, NY, NZ, OWN, LANES), bf16),
            pltpu.VMEM((NK, NY, ROWS, NX * LANES), bf16),
            pltpu.VMEM((NK, NY, ROWS, LANES), bf16),
            dma((6, NK)), dma((6, NK)), dma((NK, NZ)),
            dma((8, NK)), dma((8, NK)), dma((NK, NY)),
            dma((NK,)), dma((NK, NY + 1)),
            dma((NK,)), dma((NK, NX)),
            dma((NK,)), dma((NK, NX)),
            dma((NK,)), dma((NK,)),
            dma((NK,)), dma((NK,)),
            dma((5,)),
        ],
        compiler_params=pltpu.CompilerParams(
            collective_id=0, has_side_effects=True, vmem_limit_bytes=52 * 2**20
        ),
        name="galore_step",
    )(projector, first_moment, second_moment, activations, cotangent)
    return pl.pallas_call(
        place,
        out_shape=shapes,
        in_specs=[pl.BlockSpec(memory_space=pl.ANY)] * 3,
        out_specs=(hbm,) * 3,
        scratch_shapes=[dma((3,))],
        compiler_params=pltpu.CompilerParams(vmem_limit_bytes=16 * 2**20),
        name="place_results",
    )(*results)


def solution(mesh):
    placed = (
        P("dp", None),
        P(None, "dp", "tensor"),
        P(None, "dp", None),
        P(None, "dp", "tensor"),
        P(None, "dp", "tensor"),
    )
    return jax.shard_map(
        on_device,
        mesh=mesh,
        in_specs=placed,
        out_specs=(P(None, "dp", "tensor"), P(None, "dp", "tensor"), P(None, "dp", "tensor")),
        check_vma=False,
    )
```
